512 devices in a mesh: clip: 8 (over x, z_lo), frame: 4 (over z_hi), head: 16 (over y, core).
Axes of the slice: x: 4, y: 8, z: 8 (z_hi: 4, z_lo: 2; z = z_hi * 2 + z_lo), core: 2. Of those that a mesh axis runs over, the one named last changes fastest.
Arguments:
- residual: bfloat16 [8, 16, 32, 5120], P('clip', 'frame', None, 'head'), may hold values from -6 to 6
- projections: bfloat16 [8, 16, 32, 3, 4096], P('clip', 'frame', None, None, 'head'), may hold values from -8 to 8
- out_weight: bfloat16 [4096, 5120], P('head', 'frame'), may hold values from -0.1875 to 0.1875
- out_grad: bfloat16 [8, 16, 32, 5120], P('clip', 'frame', None, 'head'), may hold values from -6 to 6
Outputs:
- block_out: bfloat16 [8, 16, 32, 5120], P('clip', 'frame', None, 'head')
- qkv_grad: bfloat16 [8, 16, 32, 3, 4096], P('clip', 'frame', None, None, 'head')
- weight_grad: bfloat16 [4096, 5120], P('head', 'frame')
The draws below stay inside these ranges and needn't reach their ends.
All inputs are finite; a program needn't handle non-finite values.
Results may differ from the reference program's by a relative error of at most 0.02.
Values may be sent and summed in bfloat16 or wider, within the bound.
No kernel may reach another device: no remote copies, remote signals or barrier semaphores. Data moves between devices by JAX's collectives and lax.ppermute only.
A program may use at most 64 MiB of HBM per device.

```python
import jax
import jax.numpy as jnp
from jax import lax

D = 5120
HEAD_DIM = 128
FRAMES = 16
PATCHES = 32
INNER = 4096
CLIPS = 8
N_FRAME = 4
N_HEAD = 16


def draw_projections(key, part):
    key = jax.random.fold_in(key, 7)
    shape = (CLIPS, FRAMES, PATCHES, 3, INNER)
    base = jnp.clip(jax.random.normal(key, shape, jnp.float32), -6.0, 6.0)
    return base.astype(jnp.bfloat16)


def block_scale(rng, shape, split, least, high):
    loudness, own = 1.0, jax.random.fold_in(rng, 6)
    for axis_at, parts in split:
        steps = jnp.exp(jax.random.uniform(jax.random.fold_in(own, axis_at), (parts,), jnp.float32, least / len(split), high / len(split)))
        loudness = loudness * jnp.repeat(steps, shape[axis_at] // parts).reshape([-1 if axis == axis_at else 1 for axis in range(len(shape))])
    return loudness


def bell_draw(own_key, dims, spread, bound, pieces=(), held_as=jnp.bfloat16):
    gain = block_scale(own_key, dims, pieces, -0.22, 0.18) if pieces else 1.0
    entries = jax.random.normal(own_key, dims, jnp.float32) * spread * gain
    return jnp.minimum(jnp.maximum(entries, -bound), bound).astype(held_as)


def setup_inputs(seed: int = 0) -> dict:
    keys = jax.random.split(jax.random.key(seed), 5)
    residual = bell_draw(keys[0], (CLIPS, FRAMES, PATCHES, D), 1.0, 6.0, ((0, 8), (1, 4), (3, 16)))
    projections = draw_projections(jax.random.fold_in(keys[4], 71), 0)
    out_weight = bell_draw(keys[2], (INNER, D), (INNER // 4) ** -0.5, 0.1875, ((0, 16), (1, 4)))
    out_grad = bell_draw(keys[3], (CLIPS, FRAMES, PATCHES, D), 1.0, 6.0, ((0, 8), (1, 4), (3, 16)))
    return {"residual": residual, "projections": projections, "out_weight": out_weight, "out_grad": out_grad}


def attend(queries, key_rows, values):
    score_scale = queries.shape[-1] ** -0.5
    scores = jnp.einsum('cfphe,cgphe->cphfg', queries.astype(jnp.float32), key_rows.astype(jnp.float32)) * score_scale
    frame_index = jnp.arange(queries.shape[1])
    allowed = frame_index[:, None] >= frame_index[None, :]
    scores = jnp.where(allowed, scores, -jnp.inf)
    row_max = jnp.max(scores, axis=-1, keepdims=True)
    shifted = jnp.exp(scores - row_max)
    probability = shifted / jnp.sum(shifted, axis=-1, keepdims=True)
    weights = probability.astype(jnp.bfloat16)
    attended = jnp.einsum('cphfg,cgphe->cfphe', weights.astype(jnp.float32), values.astype(jnp.float32)).astype(jnp.bfloat16)
    return probability, weights, attended


def attend_back(queries, key_rows, values, probability, weights, grad_rows):
    score_scale = queries.shape[-1] ** -0.5
    prob_grad = jnp.einsum('cfphe,cgphe->cphfg', grad_rows.astype(jnp.float32), values.astype(jnp.float32))
    row_dot = jnp.sum(probability * prob_grad, axis=-1, keepdims=True)
    score_grad = (probability * (prob_grad - row_dot)).astype(jnp.bfloat16)
    query_grad = (jnp.einsum('cphfg,cgphe->cfphe', score_grad.astype(jnp.float32), key_rows.astype(jnp.float32)) * score_scale).astype(jnp.bfloat16)
    key_grad = (jnp.einsum('cphfg,cfphe->cgphe', score_grad.astype(jnp.float32), queries.astype(jnp.float32)) * score_scale).astype(jnp.bfloat16)
    value_grad = jnp.einsum('cphfg,cfphe->cgphe', weights.astype(jnp.float32), grad_rows.astype(jnp.float32)).astype(jnp.bfloat16)
    return query_grad, key_grad, value_grad


def add_head(running, pair_in):
    piece_sum = jnp.dot(pair_in[0], pair_in[1], preferred_element_type=jnp.float32).astype(jnp.bfloat16)
    piece_sum = lax.optimization_barrier(piece_sum)
    return running + piece_sum.astype(jnp.float32), None


def add_group(running, pair_in):
    piece_sum = lax.dot_general(pair_in[0], pair_in[1], (((0,), (0,)), ((), ())), preferred_element_type=jnp.float32).astype(jnp.bfloat16)
    piece_sum = lax.optimization_barrier(piece_sum)
    return running + piece_sum.astype(jnp.float32), None


def reference(residual, projections, out_weight, out_grad):
    clip_count, frames, patches, _, inner_width = projections.shape
    head_count = inner_width // HEAD_DIM
    heads_view = projections.reshape(clip_count, frames, patches, 3, head_count, HEAD_DIM)
    queries = heads_view[:, :, :, 0]
    key_rows = heads_view[:, :, :, 1]
    values = heads_view[:, :, :, 2]
    probability, weights, attended = attend(queries, key_rows, values)
    tokens = clip_count * frames * patches
    flat_rows = attended.reshape(tokens, inner_width)
    inner_block = inner_width // N_HEAD
    blocks_left = flat_rows.reshape(tokens, N_HEAD, inner_block).transpose(1, 0, 2)
    blocks_right = out_weight.reshape(N_HEAD, inner_block, D)
    projected, _ = lax.scan(add_head, jnp.zeros((tokens, D), jnp.float32), (blocks_left, blocks_right))
    block_out = (residual.reshape(tokens, D).astype(jnp.float32) + projected).astype(jnp.bfloat16).reshape(residual.shape)
    grad_flat = out_grad.reshape(tokens, D)
    attended_grad = lax.dot_general(grad_flat, out_weight, (((1,), (1,)), ((), ())), preferred_element_type=jnp.float32).astype(jnp.bfloat16)
    groups = clip_count * N_FRAME
    group_rows = tokens // groups
    grad_sum, _ = lax.scan(add_group, jnp.zeros((inner_width, D), jnp.float32), (flat_rows.reshape(groups, group_rows, inner_width), grad_flat.reshape(groups, group_rows, D)))
    weight_grad = grad_sum.astype(jnp.bfloat16)
    grad_rows = attended_grad.reshape(clip_count, frames, patches, head_count, HEAD_DIM)
    query_grad, key_grad, value_grad = attend_back(queries, key_rows, values, probability, weights, grad_rows)
    qkv_grad = jnp.stack([query_grad, key_grad, value_grad], axis=3).reshape(projections.shape)
    return block_out, qkv_grad, weight_grad
```

```python
import jax
import jax.numpy as jnp
from jax import lax
from jax.experimental import pallas as pl
from jax.experimental.pallas import tpu as pltpu
from jax.sharding import Mesh, PartitionSpec as P

HEAD_DIM = 128
AXES = ("x", "zl", "frame", "y", "core")
CLIP = ("x", "zl")
SWAP = ((0, 1), (1, 0))
F32 = jnp.float32
BF16 = jnp.bfloat16


def probabilities(queries, key_rows, patches):
    rows = queries.shape[0]
    scores = lax.dot_general(
        queries, key_rows, (((1,), (1,)), ((), ())), preferred_element_type=F32
    ) * (HEAD_DIM ** (-0.5))
    at = lax.broadcasted_iota(jnp.int32, (rows, rows), 0)
    to = lax.broadcasted_iota(jnp.int32, (rows, rows), 1)
    allowed = (at % patches == to % patches) & (at >= to)
    scores = jnp.where(allowed, scores, -jnp.inf)
    shifted = jnp.exp(scores - jnp.max(scores, axis=-1, keepdims=True))
    return shifted / jnp.sum(shifted, axis=-1, keepdims=True)


def attend_kernel(patches, qkv_ref, attended_ref):
    width = attended_ref.shape[1]
    for at in range(0, width, HEAD_DIM):
        queries = qkv_ref[:, at : at + HEAD_DIM]
        key_rows = qkv_ref[:, width + at : width + at + HEAD_DIM]
        values = qkv_ref[:, 2 * width + at : 2 * width + at + HEAD_DIM]
        weights = probabilities(queries, key_rows, patches).astype(BF16)
        attended_ref[:, at : at + HEAD_DIM] = jnp.dot(
            weights, values, preferred_element_type=F32
        ).astype(BF16)


def attend_back_kernel(patches, qkv_ref, shares_ref, grads_ref):
    width = shares_ref.shape[2]
    grad_rows = jnp.sum(shares_ref[...].astype(F32), axis=0).astype(BF16)
    score_scale = HEAD_DIM ** (-0.5)
    for at in range(0, width, HEAD_DIM):
        queries = qkv_ref[:, at : at + HEAD_DIM]
        key_rows = qkv_ref[:, width + at : width + at + HEAD_DIM]
        values = qkv_ref[:, 2 * width + at : 2 * width + at + HEAD_DIM]
        grad = grad_rows[:, at : at + HEAD_DIM]
        probability = probabilities(queries, key_rows, patches)
        prob_grad = lax.dot_general(
            grad, values, (((1,), (1,)), ((), ())), preferred_element_type=F32
        )
        row_dot = jnp.sum(probability * prob_grad, axis=-1, keepdims=True)
        score_grad = (probability * (prob_grad - row_dot)).astype(BF16)
        query_grad = jnp.dot(score_grad, key_rows, preferred_element_type=F32) * score_scale
        key_grad = (
            lax.dot_general(
                score_grad, queries, (((0,), (0,)), ((), ())), preferred_element_type=F32
            )
            * score_scale
        )
        value_grad = lax.dot_general(
            probability.astype(BF16), grad, (((0,), (0,)), ((), ())), preferred_element_type=F32
        )
        for part, value in enumerate((query_grad, key_grad, value_grad)):
            start = part * width + at
            grads_ref[:, start : start + HEAD_DIM] = value.astype(BF16)


def whole(kernel, out_shape, *operands):
    return pl.pallas_call(
        kernel,
        out_shape=out_shape,
        compiler_params=pltpu.CompilerParams(vmem_limit_bytes=32 * 1024 * 1024),
    )(*operands)


def local(residual, projections, out_weight, out_grad):
    n_frame, n_y = lax.axis_size("frame"), lax.axis_size("y")
    n_clip = lax.axis_size("x") * lax.axis_size("zl")
    core = lax.axis_index("core")
    _, steps, patches, _, inner = projections.shape
    width = out_grad.shape[-1]
    own_patches = patches // n_frame
    rows = steps * n_frame * own_patches
    tokens = steps * patches
    halves = n_y // n_frame

    weight_t = out_weight.T.reshape(halves, 2, width, inner)
    weight_keep = lax.dynamic_index_in_dim(weight_t, core, 1, keepdims=False)
    weight_give = lax.dynamic_index_in_dim(weight_t, 1 - core, 1, keepdims=False)
    weight_got = lax.ppermute(weight_give, "core", SWAP)
    first = jnp.where(core == 0, weight_keep, weight_got)
    second = jnp.where(core == 0, weight_got, weight_keep)
    weight_rows = jnp.concatenate([first, second], axis=-1).reshape(halves * width, 2 * inner)

    there = [
        (f * n_y + y, (y // halves) * n_y + halves * f + y % halves)
        for f in range(n_frame)
        for y in range(n_y)
    ]
    back = [(b, a) for a, b in there]

    grad_t = (
        out_grad.reshape(steps, n_frame, own_patches, width)
        .transpose(3, 1, 0, 2)
        .reshape(width, tokens)
    )
    grad_moved = lax.ppermute(grad_t, ("frame", "y"), back)
    grad_all = lax.all_gather(grad_moved, ("y", "core"))
    grad_all = grad_all.reshape(n_frame, halves, 2, width, tokens)

    sent = (
        projections.reshape(steps, n_frame, own_patches, 3 * inner)
        .transpose(1, 0, 2, 3)
    )
    qkv = lax.all_to_all(sent, "frame", 0, 0, tiled=True).reshape(rows, 3 * inner)
    attended = whole(
        lambda *refs: attend_kernel(own_patches, *refs),
        jax.ShapeDtypeStruct((rows, inner), BF16),
        qkv,
    )
    attended_all = lax.all_gather(attended, ("frame", "core"))
    group = tokens // n_frame
    attended_all = attended_all.reshape(n_frame, 2, n_frame, group, inner)
    feature_rows = attended_all.transpose(2, 0, 3, 1, 4).reshape(n_frame * tokens, 2 * inner)

    partial = lax.dot_general(
        weight_rows, feature_rows, (((1,), (1,)), ((), ())), preferred_element_type=F32
    ).astype(BF16)
    pieces = (
        partial.reshape(halves, width, n_frame, tokens)
        .transpose(2, 0, 1, 3)
        .reshape(n_y, width, tokens)
    )
    pieces = lax.all_to_all(pieces, "y", 0, 0, tiled=True)
    projected = jnp.sum(pieces.astype(F32), axis=0).astype(BF16)
    projected = lax.ppermute(projected, ("frame", "y"), there)
    projected = (
        projected.reshape(width, n_frame, steps, own_patches)
        .transpose(2, 1, 3, 0)
        .reshape(residual.shape)
    )
    block_out = (residual.astype(F32) + projected.astype(F32)).astype(BF16)

    grad_own = lax.dynamic_index_in_dim(grad_all, core, 2, keepdims=False)
    grad_own = grad_own.transpose(1, 2, 0, 3).reshape(halves * width, n_frame * tokens)
    share = lax.dot_general(
        grad_own, weight_rows, (((0,), (0,)), ((), ())), preferred_element_type=F32
    ).astype(BF16)
    share = (
        share.reshape(n_frame, n_frame, group, 2, inner)
        .transpose(1, 3, 0, 2, 4)
        .reshape(2 * n_frame, rows, inner)
    )
    shares = lax.all_to_all(share, ("frame", "core"), 0, 0, tiled=True)

    own_rows = lax.dynamic_index_in_dim(
        feature_rows.reshape(n_frame * tokens, 2, inner), core, 1, keepdims=False
    )
    grad_rows = grad_all.transpose(0, 4, 1, 2, 3).reshape(n_frame * tokens, -1)
    weight_part = lax.dot_general(
        own_rows, grad_rows, (((0,), (0,)), ((), ())), preferred_element_type=F32
    ).astype(BF16)
    weight_part = weight_part.reshape(n_clip, inner // n_clip, -1)
    weight_part = lax.all_to_all(weight_part, CLIP, 0, 0, tiled=True)
    weight_sum = jnp.sum(weight_part.astype(F32), axis=0).astype(BF16)
    weight_sum = jnp.broadcast_to(weight_sum[None], (n_clip, *weight_sum.shape))
    weight_grad = lax.all_to_all(weight_sum, CLIP, 0, 0, tiled=True).reshape(out_weight.shape)

    grads = whole(
        lambda *refs: attend_back_kernel(own_patches, *refs),
        jax.ShapeDtypeStruct((rows, 3 * inner), BF16),
        qkv,
        shares,
    )
    grads = grads.reshape(n_frame, steps, own_patches, 3 * inner)
    grads = lax.all_to_all(grads, "frame", 0, 0, tiled=True)
    qkv_grad = grads.transpose(1, 0, 2, 3).reshape(projections.shape)
    return (block_out, qkv_grad, weight_grad)


def solution(mesh):
    n_clip, n_frame, n_head = mesh.devices.shape
    fine = Mesh(mesh.devices.reshape(n_clip // 2, 2, n_frame, n_head // 2, 2), AXES)
    head = ("y", "core")
    in_specs = (
        P(CLIP, "frame", None, head),
        P(CLIP, "frame", None, None, head),
        P(head, "frame"),
        P(CLIP, "frame", None, head),
    )
    out_specs = (
        P(CLIP, "frame", None, head),
        P(CLIP, "frame", None, None, head),
        P(head, "frame"),
    )
    return jax.shard_map(local, mesh=fine, in_specs=in_specs, out_specs=out_specs, check_vma=False)
```

```python
import functools

import jax
import jax.numpy as jnp
from jax import lax
from jax.experimental import pallas as pl
from jax.experimental.pallas import tpu as pltpu
from jax.sharding import Mesh, PartitionSpec as P

HEAD_DIM = 128
AXES = ("x", "zl", "frame", "y", "core")
CLIP = ("x", "zl")
SWAP = ((0, 1), (1, 0))
F32 = jnp.float32
BF16 = jnp.bfloat16


def probabilities(queries, key_rows, patches):
    rows = queries.shape[0]
    scores = lax.dot_general(
        queries, key_rows, (((1,), (1,)), ((), ())), preferred_element_type=F32
    ) * (HEAD_DIM ** (-0.5))
    at = lax.broadcasted_iota(jnp.int32, (rows, rows), 0)
    to = lax.broadcasted_iota(jnp.int32, (rows, rows), 1)
    allowed = (at % patches == to % patches) & (at >= to)
    scores = jnp.where(allowed, scores, -jnp.inf)
    shifted = jnp.exp(scores - jnp.max(scores, axis=-1, keepdims=True))
    return shifted / jnp.sum(shifted, axis=-1, keepdims=True)


def attend_kernel(place_ref, all_ref, rows_ref, own_ref, sums_ref):
    n, tokens = rows_ref.shape[0], rows_ref.shape[1]
    frames, _, patches, width = all_ref.shape
    group = patches // n
    for at in range(0, width, HEAD_DIM):
        features = slice(at, at + HEAD_DIM)
        whole_parts = [all_ref[:, part, :, features].astype(F32) for part in range(3)]
        for index in range(n):
            span = slice(index * group, (index + 1) * group)
            blocks = [
                part[:, span].reshape(frames * group, HEAD_DIM).astype(BF16)
                for part in whole_parts
            ]
            queries, key_rows, values = blocks

            @pl.when(place_ref[0] == index)
            def _():
                for part, block in enumerate(blocks):
                    own_ref[part, :, features] = block

            weights = probabilities(queries, key_rows, group).astype(BF16)
            attended = jnp.dot(weights, values, preferred_element_type=F32)
            sums_ref[:, span, features] = attended.reshape(frames, group, HEAD_DIM)
    rows_ref[...] = sums_ref[...].reshape(n, tokens, width).astype(BF16)


def project_block(weight, rows):
    flat = rows.reshape(-1, rows.shape[-1])
    return lax.dot_general(weight, flat, (((1,), (1,)), ((), ())), preferred_element_type=F32)


def project_other_kernel(place_ref, weight_ref, rows_ref, pieces_ref):
    n, tokens = rows_ref.shape[0], rows_ref.shape[1]
    halves = weight_ref.shape[0]
    for half in range(halves):
        block = project_block(weight_ref[half, 1 - place_ref[1]], rows_ref[...]).astype(BF16)
        for frame in range(n):
            pieces_ref[frame * halves + half] = block[:, frame * tokens : (frame + 1) * tokens]


def project_own_kernel(place_ref, weight_ref, rows_ref, got_ref, pieces_ref):
    n, tokens = rows_ref.shape[0], rows_ref.shape[1]
    halves = weight_ref.shape[0]
    for half in range(halves):
        block = project_block(weight_ref[half, place_ref[1]], rows_ref[...])
        for frame in range(n):
            at = frame * halves + half
            piece = block[:, frame * tokens : (frame + 1) * tokens] + got_ref[at].astype(F32)
            pieces_ref[at] = piece.astype(BF16)


def attended_grad_kernel(place_ref, weight_ref, own_ref, other_ref, shares_ref, sums_ref):
    n, step = shares_ref.shape[0], shares_ref.shape[1] // shares_ref.shape[0]
    halves = weight_ref.shape[0]
    core = place_ref[1]
    frames, patches, width = sums_ref.shape
    group = patches // n
    for frame in range(n):
        total = None
        for half in range(halves):
            for grads, at in ((own_ref, core), (other_ref, 1 - core)):
                term = lax.dot_general(
                    grads[frame * halves + half],
                    weight_ref[half, at],
                    (((0,), (0,)), ((), ())),
                    preferred_element_type=F32,
                )
                total = term if total is None else total + term
        sums_ref[...] = total.reshape(sums_ref.shape)
        for j in range(n):
            start = pl.multiple_of(lax.rem(place_ref[0] + j, n) * group, group)
            share = sums_ref[:, pl.ds(start, group), :].reshape(step, width)
            shares_ref[j, frame * step : (frame + 1) * step, :] = share.astype(BF16)


def weight_grad_kernel(place_ref, rows_ref, own_ref, other_ref, out_ref, sums_ref):
    n = rows_ref.shape[0]
    halves = sums_ref.shape[0]
    core = place_ref[1]
    for half in range(halves):
        for grads, at in ((own_ref, core), (other_ref, 1 - core)):
            total = None
            for frame in range(n):
                term = jnp.dot(
                    grads[frame * halves + half], rows_ref[frame], preferred_element_type=F32
                )
                total = term if total is None else total + term
            sums_ref[half, at] = total
    out_ref[...] = sums_ref[...].reshape(-1, sums_ref.shape[-1]).T.astype(BF16)


def attend_back_kernel(patches, place_ref, qkv_ref, *refs):
    shares, (out_ref, grads_ref) = refs[:-2], refs[-2:]
    width = shares[0].shape[1]
    grad_rows = shares[0][...].astype(F32)
    for share in shares[1:]:
        grad_rows = grad_rows + share[...].astype(F32)
    grad_rows = grad_rows.astype(BF16)
    score_scale = HEAD_DIM ** (-0.5)
    for at in range(0, width, HEAD_DIM):
        queries = qkv_ref[0, :, at : at + HEAD_DIM]
        key_rows = qkv_ref[1, :, at : at + HEAD_DIM]
        values = qkv_ref[2, :, at : at + HEAD_DIM]
        grad = grad_rows[:, at : at + HEAD_DIM]
        probability = probabilities(queries, key_rows, patches)
        prob_grad = lax.dot_general(
            grad, values, (((1,), (1,)), ((), ())), preferred_element_type=F32
        )
        row_dot = jnp.sum(probability * prob_grad, axis=-1, keepdims=True)
        score_grad = (probability * (prob_grad - row_dot)).astype(BF16)
        query_grad = jnp.dot(score_grad, key_rows, preferred_element_type=F32) * score_scale
        key_grad = (
            lax.dot_general(
                score_grad, queries, (((0,), (0,)), ((), ())), preferred_element_type=F32
            )
            * score_scale
        )
        value_grad = lax.dot_general(
            probability.astype(BF16), grad, (((0,), (0,)), ((), ())), preferred_element_type=F32
        )
        for part, value in enumerate((query_grad, key_grad, value_grad)):
            grads_ref[part, :, at : at + HEAD_DIM] = value.astype(BF16)
    n, step = out_ref.shape[0], out_ref.shape[2]
    for j in range(n):
        start = pl.multiple_of(lax.rem(place_ref[0] + j, n) * step, step)
        out_ref[j] = grads_ref[:, pl.ds(start, step), :]


def arrange_kernel(place_ref, *refs):
    parts, (out_ref, sums_ref) = refs[:-2], refs[-2:]
    n = len(parts)
    frames, kinds, patches, width = out_ref.shape
    group = patches // n
    for j, part in enumerate(parts):
        start = pl.multiple_of(lax.rem(place_ref[0] + (n - j), n) * group, group)
        for kind in range(kinds):
            rows = part[kind].astype(F32).reshape(frames, group, width)
            sums_ref[:, kind, pl.ds(start, group), :] = rows
    out_ref[...] = sums_ref[...].astype(BF16)


def whole(kernel, out_shape, place, *operands, scratch=(), flops=0):
    several = isinstance(out_shape, (list, tuple))
    moved = sum(o.size * o.dtype.itemsize for o in operands)
    return pl.pallas_call(
        kernel,
        out_shape=out_shape,
        in_specs=[pl.BlockSpec(memory_space=pltpu.SMEM)]
        + [pl.BlockSpec(memory_space=pltpu.VMEM)] * len(operands),
        out_specs=[pl.BlockSpec(memory_space=pltpu.VMEM)] * len(out_shape)
        if several
        else pl.BlockSpec(memory_space=pltpu.VMEM),
        scratch_shapes=list(scratch),
        compiler_params=pltpu.CompilerParams(vmem_limit_bytes=32 * 1024 * 1024),
        cost_estimate=pl.CostEstimate(flops=flops, bytes_accessed=2 * moved, transcendentals=0),
    )(place, *operands)


def shifted(array, by, axis):
    n = lax.axis_size(axis)
    return lax.ppermute(array, axis, [(i, (i + by) % n) for i in range(n)])


def copies(array, n):
    return jnp.broadcast_to(array[None], (n, *array.shape))


def local(residual, projections, out_weight, out_grad):
    n_frame, n_y = lax.axis_size("frame"), lax.axis_size("y")
    n_clip = lax.axis_size("x") * lax.axis_size("zl")
    frame, core = lax.axis_index("frame"), lax.axis_index("core")
    place = jnp.stack([frame, core]).astype(jnp.int32)
    _, steps, patches, kinds, inner = projections.shape
    width = out_grad.shape[-1]
    frames = steps * n_frame
    step = steps * (patches // n_frame)
    rows = step * n_frame
    tokens = steps * patches
    halves = n_y // n_frame
    product = 2 * n_frame * tokens * inner * width * halves

    there = [
        (f * n_y + y, (y // halves) * n_y + halves * f + y % halves)
        for f in range(n_frame)
        for y in range(n_y)
    ]
    back = [(b, a) for a, b in there]

    grad_moved = lax.ppermute(out_grad.reshape(tokens, width).T, ("frame", "y"), back)
    qkv_all = lax.all_gather(
        projections.reshape(projections.shape[1:]).transpose(0, 2, 1, 3), "frame", tiled=True
    )
    grad_own = lax.all_to_all(copies(grad_moved, n_y), "y", 0, 0, tiled=True)
    grad_other = lax.ppermute(grad_own, "core", SWAP)

    feature_rows, qkv = whole(
        attend_kernel,
        [
            jax.ShapeDtypeStruct((n_frame, tokens, inner), BF16),
            jax.ShapeDtypeStruct((kinds, rows, inner), BF16),
        ],
        place,
        qkv_all,
        scratch=[pltpu.VMEM((frames, patches, inner), F32)],
        flops=product,
    )

    weight_t = out_weight.T.reshape(halves, 2, width, inner)
    piece_shape = jax.ShapeDtypeStruct((n_y, width, tokens), BF16)
    pieces_other = whole(
        project_other_kernel, piece_shape, place, weight_t, feature_rows, flops=product
    )
    pieces_got = lax.ppermute(pieces_other, "core", SWAP)
    pieces = whole(
        project_own_kernel, piece_shape, place, weight_t, feature_rows, pieces_got, flops=product
    )
    pieces, grad_own, grad_other = lax.optimization_barrier((pieces, grad_own, grad_other))
    pieces = lax.all_to_all(pieces, "y", 0, 0, tiled=True)

    shares = whole(
        attended_grad_kernel,
        jax.ShapeDtypeStruct((n_frame, rows, inner), BF16),
        place,
        weight_t,
        grad_own,
        grad_other,
        scratch=[pltpu.VMEM((steps, patches, inner), F32)],
        flops=2 * product,
    )
    weight_part = whole(
        weight_grad_kernel,
        jax.ShapeDtypeStruct(out_weight.shape, BF16),
        place,
        feature_rows,
        grad_own,
        grad_other,
        scratch=[pltpu.VMEM((halves, 2, width, inner), F32)],
        flops=2 * product,
    )
    shares = [shares[0]] + [shifted(shares[j], j, "frame") for j in range(1, n_frame)]
    grads = whole(
        functools.partial(attend_back_kernel, patches // n_frame),
        jax.ShapeDtypeStruct((n_frame, kinds, step, inner), BF16),
        place,
        qkv,
        *shares,
        scratch=[pltpu.VMEM((kinds, rows, inner), BF16)],
    )

    weight_part, _, pieces = lax.optimization_barrier((weight_part, grads, pieces))
    weight_part = weight_part.reshape(n_clip, inner // n_clip, -1)
    weight_part = lax.all_to_all(weight_part, CLIP, 0, 0, tiled=True)
    projected = jnp.sum(pieces.astype(F32), axis=0).astype(BF16)
    grads = [grads[0]] + [shifted(grads[j], j, "frame") for j in range(1, n_frame)]

    weight_sum = jnp.sum(weight_part.astype(F32), axis=0).astype(BF16)
    weight_sum, _ = lax.optimization_barrier((weight_sum, grads))
    weight_grad = lax.all_to_all(copies(weight_sum, n_clip), CLIP, 0, 0, tiled=True)
    weight_grad = weight_grad.reshape(out_weight.shape)

    projected = lax.ppermute(projected, ("frame", "y"), there)
    projected = projected.T.reshape(residual.shape)
    block_out = (residual.astype(F32) + projected.astype(F32)).astype(BF16)
    qkv_grad = whole(
        arrange_kernel,
        jax.ShapeDtypeStruct((steps, kinds, patches, inner), BF16),
        place,
        *grads,
        scratch=[pltpu.VMEM((steps, kinds, patches, inner), F32)],
    )
    qkv_grad = qkv_grad.transpose(0, 2, 1, 3).reshape(projections.shape)
    return (block_out, qkv_grad, weight_grad)


def solution(mesh):
    n_clip, n_frame, n_head = mesh.devices.shape
    fine = Mesh(mesh.devices.reshape(n_clip // 2, 2, n_frame, n_head // 2, 2), AXES)
    head = ("y", "core")
    in_specs = (
        P(CLIP, "frame", None, head),
        P(CLIP, "frame", None, None, head),
        P(head, "frame"),
        P(CLIP, "frame", None, head),
    )
    out_specs = (
        P(CLIP, "frame", None, head),
        P(CLIP, "frame", None, None, head),
        P(head, "frame"),
    )
    return jax.shard_map(local, mesh=fine, in_specs=in_specs, out_specs=out_specs, check_vma=False)
```

```python
import jax
import jax.numpy as jnp
from jax import lax
from jax.experimental import pallas as pl
from jax.experimental.pallas import tpu as pltpu
from jax.sharding import Mesh, PartitionSpec as P

HEAD_DIM = 128
AXES = ("x", "zl", "frame", "y", "core")
CLIP = ("x", "zl")
SWAP = ((0, 1), (1, 0))
F32 = jnp.float32
BF16 = jnp.bfloat16


def probabilities(queries, key_rows, patches):
    rows = queries.shape[0]
    scores = lax.dot_general(
        queries, key_rows, (((1,), (1,)), ((), ())), preferred_element_type=F32
    ) * (HEAD_DIM ** (-0.5))
    at = lax.broadcasted_iota(jnp.int32, (rows, rows), 0)
    to = lax.broadcasted_iota(jnp.int32, (rows, rows), 1)
    allowed = (at % patches == to % patches) & (at >= to)
    scores = jnp.where(allowed, scores, -jnp.inf)
    shifted = jnp.exp(scores - jnp.max(scores, axis=-1, keepdims=True))
    return shifted / jnp.sum(shifted, axis=-1, keepdims=True)


def block_of(part):
    return part.reshape(-1, part.shape[-1]).astype(BF16)


def attend_kernel(all_ref, rows_ref, sums_ref):
    n, tokens = rows_ref.shape[0], rows_ref.shape[1]
    frames, kinds, patches, width = all_ref.shape
    group = patches // n
    for at in range(0, width, HEAD_DIM):
        features = slice(at, at + HEAD_DIM)
        parts = [all_ref[:, kind, :, features].astype(F32) for kind in range(kinds)]
        for start in range(0, patches, group):
            span = slice(start, start + group)
            queries, key_rows, values = (block_of(part[:, span]) for part in parts)
            weights = probabilities(queries, key_rows, group).astype(BF16)
            attended = jnp.dot(weights, values, preferred_element_type=F32)
            sums_ref[:, span, features] = attended.reshape(frames, group, HEAD_DIM)
    rows_ref[...] = sums_ref[...].reshape(n, tokens, width).astype(BF16)


def slot(place_ref, frame, n):
    return lax.rem(2 * place_ref[0] + n // 2 + n - frame, n)


def project_block(weight, rows):
    flat = rows.reshape(-1, rows.shape[-1])
    return lax.dot_general(weight, flat, (((1,), (1,)), ((), ())), preferred_element_type=F32)


def project_other_kernel(place_ref, weight_ref, rows_ref, pieces_ref):
    n, tokens = rows_ref.shape[0], rows_ref.shape[1]
    halves = weight_ref.shape[0]
    for half in range(halves):
        block = project_block(weight_ref[half, 1 - place_ref[1]], rows_ref[...]).astype(BF16)
        for frame in range(n):
            pieces_ref[slot(place_ref, frame, n) * halves + half] = block[:, frame * tokens : (frame + 1) * tokens]


def project_own_kernel(place_ref, weight_ref, rows_ref, got_ref, pieces_ref):
    n, tokens = rows_ref.shape[0], rows_ref.shape[1]
    halves = weight_ref.shape[0]
    for half in range(halves):
        block = project_block(weight_ref[half, place_ref[1]], rows_ref[...])
        for frame in range(n):
            at = slot(place_ref, frame, n) * halves + half
            piece = block[:, frame * tokens : (frame + 1) * tokens] + got_ref[at].astype(F32)
            pieces_ref[at] = piece.astype(BF16)


def attended_grad_kernel(place_ref, weight_ref, own_ref, other_ref, out_ref):
    n, halves = out_ref.shape[0], weight_ref.shape[0]
    core = place_ref[1]
    for frame in range(n):
        total = None
        for half in range(halves):
            for grads, at in ((own_ref, core), (other_ref, 1 - core)):
                term = lax.dot_general(
                    grads[slot(place_ref, frame, n) * halves + half],
                    weight_ref[half, at],
                    (((0,), (0,)), ((), ())),
                    preferred_element_type=F32,
                )
                total = term if total is None else total + term
        out_ref[frame] = total.astype(BF16)


def weight_grad_kernel(place_ref, rows_ref, own_ref, other_ref, out_ref, sums_ref):
    n = rows_ref.shape[0]
    halves = sums_ref.shape[0]
    core = place_ref[1]
    for half in range(halves):
        for grads, at in ((own_ref, core), (other_ref, 1 - core)):
            total = None
            for frame in range(n):
                term = jnp.dot(
                    grads[slot(place_ref, frame, n) * halves + half], rows_ref[frame], preferred_element_type=F32
                )
                total = term if total is None else total + term
            sums_ref[half, at] = total
    out_ref[...] = sums_ref[...].reshape(-1, sums_ref.shape[-1]).T.astype(BF16)


def sum_kernel(parts_ref, out_ref):
    total = parts_ref[0].astype(F32)
    for at in range(1, parts_ref.shape[0]):
        total = total + parts_ref[at].astype(F32)
    out_ref[...] = total.astype(BF16)


def attend_back_kernel(group, place_ref, all_ref, near_ref, far_ref, out_ref, grads_ref, sums_ref):
    frames, kinds, patches, width = all_ref.shape
    steps = out_ref.shape[0]
    total = near_ref[...].astype(F32) + far_ref[...].astype(F32)
    grads_ref[...] = total.reshape(frames, patches, width)
    score_scale = HEAD_DIM ** (-0.5)
    for at in range(0, width, HEAD_DIM):
        features = slice(at, at + HEAD_DIM)
        parts = [all_ref[:, kind, :, features].astype(F32) for kind in range(kinds)]
        for start in range(0, patches, group):
            span = slice(start, start + group)
            queries, key_rows, values = (block_of(part[:, span]) for part in parts)
            grad = block_of(grads_ref[:, span, features])
            probability = probabilities(queries, key_rows, group)
            prob_grad = lax.dot_general(
                grad, values, (((1,), (1,)), ((), ())), preferred_element_type=F32
            )
            row_dot = jnp.sum(probability * prob_grad, axis=-1, keepdims=True)
            score_grad = (probability * (prob_grad - row_dot)).astype(BF16)
            query_grad = jnp.dot(score_grad, key_rows, preferred_element_type=F32) * score_scale
            key_grad = (
                lax.dot_general(
                    score_grad, queries, (((0,), (0,)), ((), ())), preferred_element_type=F32
                )
                * score_scale
            )
            value_grad = lax.dot_general(
                probability.astype(BF16), grad, (((0,), (0,)), ((), ())), preferred_element_type=F32
            )
            for kind, value in enumerate((query_grad, key_grad, value_grad)):
                sums_ref[:, kind, span, features] = value.reshape(frames, group, HEAD_DIM)
    for step in range(steps):
        out_ref[step] = sums_ref[place_ref[0] * steps + step].astype(BF16)


def whole(kernel, out_shape, place, *operands, scratch=(), flops=0):
    several = isinstance(out_shape, (list, tuple))
    moved = sum(o.size * o.dtype.itemsize for o in operands)
    return pl.pallas_call(
        kernel,
        out_shape=out_shape,
        in_specs=[pl.BlockSpec(memory_space=pltpu.SMEM)]
        + [pl.BlockSpec(memory_space=pltpu.VMEM)] * len(operands),
        out_specs=[pl.BlockSpec(memory_space=pltpu.VMEM)] * len(out_shape)
        if several
        else pl.BlockSpec(memory_space=pltpu.VMEM),
        scratch_shapes=list(scratch),
        compiler_params=pltpu.CompilerParams(vmem_limit_bytes=32 * 1024 * 1024),
        cost_estimate=pl.CostEstimate(flops=flops, bytes_accessed=2 * moved, transcendentals=0),
    )(place, *operands)


def shifted(array, by, axis):
    n = lax.axis_size(axis)
    return lax.ppermute(array, axis, [(i, (i + by) % n) for i in range(n)])


def copies(array, n):
    return jnp.broadcast_to(array[None], (n, *array.shape))


def local(residual, projections, out_weight, out_grad):
    n_frame, n_y = lax.axis_size("frame"), lax.axis_size("y")
    n_clip = lax.axis_size("x") * lax.axis_size("zl")
    frame, core = lax.axis_index("frame"), lax.axis_index("core")
    place = jnp.stack([frame, core]).astype(jnp.int32)
    _, steps, patches, kinds, inner = projections.shape
    width = out_grad.shape[-1]
    frames = steps * n_frame
    tokens = steps * patches
    halves = n_y // n_frame
    product = 2 * n_frame * tokens * inner * width * halves

    there = [
        (
            f * n_y + y,
            (2 * f + n_frame // 2 - y // halves) % n_frame * n_y + halves * f + y % halves,
        )
        for f in range(n_frame)
        for y in range(n_y)
    ]
    back = [(b, a) for a, b in there]

    grad_moved = lax.ppermute(out_grad.reshape(tokens, width).T, ("frame", "y"), back)
    qkv_all = lax.all_gather(
        projections.reshape(projections.shape[1:]).transpose(0, 2, 1, 3), "frame", tiled=True
    )
    grad_own = lax.all_to_all(copies(grad_moved, n_y), "y", 0, 0, tiled=True)
    grad_other = lax.ppermute(grad_own, "core", SWAP)

    feature_rows = pl.pallas_call(
        attend_kernel,
        out_shape=jax.ShapeDtypeStruct((n_frame, tokens, inner), BF16),
        scratch_shapes=[pltpu.VMEM((frames, patches, inner), F32)],
        compiler_params=pltpu.CompilerParams(vmem_limit_bytes=32 * 1024 * 1024),
        cost_estimate=pl.CostEstimate(flops=product, bytes_accessed=2**22, transcendentals=0),
    )(qkv_all)

    weight_t = out_weight.T.reshape(halves, 2, width, inner)
    piece_shape = jax.ShapeDtypeStruct((n_y, width, tokens), BF16)
    pieces_other = whole(
        project_other_kernel, piece_shape, place, weight_t, feature_rows, flops=product
    )
    pieces_got = lax.ppermute(pieces_other, "core", SWAP)
    pieces = whole(
        project_own_kernel, piece_shape, place, weight_t, feature_rows, pieces_got, flops=product
    )
    pieces, grad_own, grad_other = lax.optimization_barrier((pieces, grad_own, grad_other))
    pieces = lax.all_to_all(pieces, "y", 0, 0, tiled=True)

    share = whole(
        attended_grad_kernel,
        jax.ShapeDtypeStruct((n_frame, tokens, inner), BF16),
        place,
        weight_t,
        grad_own,
        grad_other,
        flops=2 * product,
    )
    weight_part = whole(
        weight_grad_kernel,
        jax.ShapeDtypeStruct(out_weight.shape, BF16),
        place,
        feature_rows,
        grad_own,
        grad_other,
        scratch=[pltpu.VMEM((halves, 2, width, inner), F32)],
        flops=2 * product,
    )
    near = lax.ppermute(share, "frame", [(i, i ^ 1) for i in range(n_frame)])
    weight_part, near = lax.optimization_barrier((weight_part, near))
    near = (share.astype(F32) + near.astype(F32)).astype(BF16)
    far = lax.ppermute(near, "frame", [(i, n_frame - 1 - i) for i in range(n_frame)])

    weight_part, _, pieces = lax.optimization_barrier((weight_part, near, pieces))
    weight_part = weight_part.reshape(n_clip, inner // n_clip, -1)
    weight_part = lax.all_to_all(weight_part, CLIP, 0, 0, tiled=True)
    projected = pl.pallas_call(
        sum_kernel,
        out_shape=jax.ShapeDtypeStruct(pieces.shape[1:], BF16),
        cost_estimate=pl.CostEstimate(flops=product, bytes_accessed=2**20, transcendentals=0),
    )(pieces)
    projected = lax.ppermute(projected, ("frame", "y"), there)

    weight_sum = jnp.sum(weight_part.astype(F32), axis=0).astype(BF16)
    _, near, projected = lax.optimization_barrier((weight_sum, near, projected))
    weight_grad = lax.all_to_all(copies(weight_sum, n_clip), CLIP, 0, 0, tiled=True)
    weight_grad = weight_grad.reshape(out_weight.shape)

    projected = projected.T.reshape(residual.shape)
    block_out = (residual.astype(F32) + projected.astype(F32)).astype(BF16)
    qkv_grad = whole(
        lambda *refs: attend_back_kernel(patches // n_frame, *refs),
        jax.ShapeDtypeStruct((steps, kinds, patches, inner), BF16),
        place,
        qkv_all,
        near,
        far,
        scratch=[
            pltpu.VMEM((frames, patches, inner), F32),
            pltpu.VMEM((frames, kinds, patches, inner), F32),
        ],
        flops=400 * product,
    )
    qkv_grad = qkv_grad.transpose(0, 2, 1, 3).reshape(projections.shape)
    return (block_out, qkv_grad, weight_grad)


def solution(mesh):
    n_clip, n_frame, n_head = mesh.devices.shape
    fine = Mesh(mesh.devices.reshape(n_clip // 2, 2, n_frame, n_head // 2, 2), AXES)
    head = ("y", "core")
    in_specs = (
        P(CLIP, "frame", None, head),
        P(CLIP, "frame", None, None, head),
        P(head, "frame"),
        P(CLIP, "frame", None, head),
    )
    out_specs = (
        P(CLIP, "frame", None, head),
        P(CLIP, "frame", None, None, head),
        P(head, "frame"),
    )
    return jax.shard_map(local, mesh=fine, in_specs=in_specs, out_specs=out_specs, check_vma=False)
```

```python
import jax
import jax.numpy as jnp
from jax import lax
from jax.experimental import pallas as pl
from jax.experimental.pallas import tpu as pltpu
from jax.sharding import Mesh, PartitionSpec as P

HEAD_DIM = 128
AXES = ("x", "zl", "frame", "y", "core")
CLIP = ("x", "zl")
SWAP = ((0, 1), (1, 0))
F32 = jnp.float32
BF16 = jnp.bfloat16


def probabilities(queries, key_rows, patches):
    rows = queries.shape[0]
    scores = lax.dot_general(
        queries, key_rows, (((1,), (1,)), ((), ())), preferred_element_type=F32
    ) * (HEAD_DIM ** (-0.5))
    at = lax.broadcasted_iota(jnp.int32, (rows, rows), 0)
    to = lax.broadcasted_iota(jnp.int32, (rows, rows), 1)
    allowed = (at % patches == to % patches) & (at >= to)
    scores = jnp.where(allowed, scores, -jnp.inf)
    shifted = jnp.exp(scores - jnp.max(scores, axis=-1, keepdims=True))
    return shifted / jnp.sum(shifted, axis=-1, keepdims=True)


def block_of(part):
    return part.reshape(-1, part.shape[-1]).astype(BF16)


def attend_kernel(all_ref, rows_ref, sums_ref):
    n, tokens = rows_ref.shape[0], rows_ref.shape[1]
    frames, kinds, patches, width = all_ref.shape
    group = patches // n
    for at in range(0, width, HEAD_DIM):
        features = slice(at, at + HEAD_DIM)
        parts = [all_ref[:, kind, :, features].astype(F32) for kind in range(kinds)]
        for start in range(0, patches, group):
            span = slice(start, start + group)
            queries, key_rows, values = (block_of(part[:, span]) for part in parts)
            weights = probabilities(queries, key_rows, group).astype(BF16)
            attended = jnp.dot(weights, values, preferred_element_type=F32)
            sums_ref[:, span, features] = attended.reshape(frames, group, HEAD_DIM)
    rows_ref[...] = sums_ref[...].reshape(n, tokens, width).astype(BF16)


def slot(place_ref, frame, n):
    return lax.rem(2 * place_ref[0] + n // 2 + n - frame, n)


def project_block(weight, rows):
    flat = rows.reshape(-1, rows.shape[-1])
    return lax.dot_general(weight, flat, (((1,), (1,)), ((), ())), preferred_element_type=F32)


def project_other_kernel(place_ref, weight_ref, rows_ref, pieces_ref):
    n, tokens = rows_ref.shape[0], rows_ref.shape[1]
    halves = weight_ref.shape[0]
    for half in range(halves):
        block = project_block(weight_ref[half, 1 - place_ref[1]], rows_ref[...]).astype(BF16)
        for frame in range(n):
            pieces_ref[slot(place_ref, frame, n) * halves + half] = block[:, frame * tokens : (frame + 1) * tokens]


def project_own_kernel(place_ref, weight_ref, rows_ref, got_ref, pieces_ref):
    n, tokens = rows_ref.shape[0], rows_ref.shape[1]
    halves = weight_ref.shape[0]
    for half in range(halves):
        block = project_block(weight_ref[half, place_ref[1]], rows_ref[...])
        for frame in range(n):
            at = slot(place_ref, frame, n) * halves + half
            piece = block[:, frame * tokens : (frame + 1) * tokens] + got_ref[at].astype(F32)
            pieces_ref[at] = piece.astype(BF16)


def attended_grad_kernel(place_ref, weight_ref, own_ref, other_ref, out_ref):
    n, halves = out_ref.shape[0], weight_ref.shape[0]
    core = place_ref[1]
    for frame in range(n):
        total = None
        for half in range(halves):
            for grads, at in ((own_ref, core), (other_ref, 1 - core)):
                term = lax.dot_general(
                    grads[slot(place_ref, frame, n) * halves + half],
                    weight_ref[half, at],
                    (((0,), (0,)), ((), ())),
                    preferred_element_type=F32,
                )
                total = term if total is None else total + term
        out_ref[frame] = total.astype(BF16)


def weight_grad_kernel(place_ref, rows_ref, own_ref, other_ref, out_ref, sums_ref):
    n = rows_ref.shape[0]
    halves = sums_ref.shape[0]
    core = place_ref[1]
    for half in range(halves):
        for grads, at in ((own_ref, core), (other_ref, 1 - core)):
            total = None
            for frame in range(n):
                term = jnp.dot(
                    grads[slot(place_ref, frame, n) * halves + half], rows_ref[frame], preferred_element_type=F32
                )
                total = term if total is None else total + term
            sums_ref[half, at] = total
    out_ref[...] = sums_ref[...].reshape(-1, sums_ref.shape[-1]).T.astype(BF16)


def sum_kernel(parts_ref, out_ref):
    total = parts_ref[0].astype(F32)
    for at in range(1, parts_ref.shape[0]):
        total = total + parts_ref[at].astype(F32)
    out_ref[...] = total.astype(BF16)


def attend_back_kernel(group, place_ref, all_ref, near_ref, far_ref, out_ref, grads_ref, sums_ref):
    frames, kinds, patches, width = all_ref.shape
    steps = out_ref.shape[0]
    total = near_ref[...].astype(F32) + far_ref[...].astype(F32)
    grads_ref[...] = total.reshape(frames, patches, width)
    score_scale = HEAD_DIM ** (-0.5)
    for at in range(0, width, HEAD_DIM):
        features = slice(at, at + HEAD_DIM)
        parts = [all_ref[:, kind, :, features].astype(F32) for kind in range(kinds)]
        for start in range(0, patches, group):
            span = slice(start, start + group)
            queries, key_rows, values = (block_of(part[:, span]) for part in parts)
            grad = block_of(grads_ref[:, span, features])
            probability = probabilities(queries, key_rows, group)
            prob_grad = lax.dot_general(
                grad, values, (((1,), (1,)), ((), ())), preferred_element_type=F32
            )
            row_dot = jnp.sum(probability * prob_grad, axis=-1, keepdims=True)
            score_grad = (probability * (prob_grad - row_dot)).astype(BF16)
            query_grad = jnp.dot(score_grad, key_rows, preferred_element_type=F32) * score_scale
            key_grad = (
                lax.dot_general(
                    score_grad, queries, (((0,), (0,)), ((), ())), preferred_element_type=F32
                )
                * score_scale
            )
            value_grad = lax.dot_general(
                probability.astype(BF16), grad, (((0,), (0,)), ((), ())), preferred_element_type=F32
            )
            for kind, value in enumerate((query_grad, key_grad, value_grad)):
                sums_ref[:, kind, span, features] = value.reshape(frames, group, HEAD_DIM)
    for step in range(steps):
        out_ref[step] = sums_ref[place_ref[0] * steps + step].astype(BF16)


def whole(kernel, out_shape, place, *operands, scratch=(), flops=0):
    several = isinstance(out_shape, (list, tuple))
    moved = sum(o.size * o.dtype.itemsize for o in operands)
    return pl.pallas_call(
        kernel,
        out_shape=out_shape,
        in_specs=[pl.BlockSpec(memory_space=pltpu.SMEM)]
        + [pl.BlockSpec(memory_space=pltpu.VMEM)] * len(operands),
        out_specs=[pl.BlockSpec(memory_space=pltpu.VMEM)] * len(out_shape)
        if several
        else pl.BlockSpec(memory_space=pltpu.VMEM),
        scratch_shapes=list(scratch),
        compiler_params=pltpu.CompilerParams(vmem_limit_bytes=16 * 1024 * 1024),
        cost_estimate=pl.CostEstimate(flops=flops, bytes_accessed=2 * moved, transcendentals=0),
    )(place, *operands)


def shifted(array, by, axis):
    n = lax.axis_size(axis)
    return lax.ppermute(array, axis, [(i, (i + by) % n) for i in range(n)])


def copies(array, n):
    return jnp.broadcast_to(array[None], (n, *array.shape))


def local(residual, projections, out_weight, out_grad):
    n_frame, n_y = lax.axis_size("frame"), lax.axis_size("y")
    n_clip = lax.axis_size("x") * lax.axis_size("zl")
    frame, core = lax.axis_index("frame"), lax.axis_index("core")
    place = jnp.stack([frame, core]).astype(jnp.int32)
    _, steps, patches, kinds, inner = projections.shape
    width = out_grad.shape[-1]
    frames = steps * n_frame
    tokens = steps * patches
    halves = n_y // n_frame
    product = 2 * n_frame * tokens * inner * width * halves

    there = [
        (
            f * n_y + y,
            (2 * f + n_frame // 2 - y // halves) % n_frame * n_y + halves * f + y % halves,
        )
        for f in range(n_frame)
        for y in range(n_y)
    ]
    back = [(b, a) for a, b in there]

    grad_moved = lax.ppermute(out_grad.reshape(tokens, width).T, ("frame", "y"), back)
    qkv_all = lax.all_gather(
        projections.reshape(projections.shape[1:]).transpose(0, 2, 1, 3), "frame", tiled=True
    )
    grad_moved, qkv_all = lax.optimization_barrier((grad_moved, qkv_all))
    grad_own = lax.all_to_all(copies(grad_moved, n_y), "y", 0, 0, tiled=True)

    feature_rows = pl.pallas_call(
        attend_kernel,
        out_shape=jax.ShapeDtypeStruct((n_frame, tokens, inner), BF16),
        scratch_shapes=[pltpu.VMEM((frames, patches, inner), F32)],
        compiler_params=pltpu.CompilerParams(vmem_limit_bytes=16 * 1024 * 1024),
        cost_estimate=pl.CostEstimate(flops=product, bytes_accessed=2**22, transcendentals=0),
    )(qkv_all)

    weight_t = out_weight.T.reshape(halves, 2, width, inner)
    piece_shape = jax.ShapeDtypeStruct((n_y, width, tokens), BF16)
    pieces_other = whole(
        project_other_kernel, piece_shape, place, weight_t, feature_rows, flops=product
    )
    pieces_got = lax.ppermute(pieces_other, "core", SWAP)
    pieces = whole(
        project_own_kernel, piece_shape, place, weight_t, feature_rows, pieces_got, flops=product
    )
    pieces, grad_own = lax.optimization_barrier((pieces, grad_own))
    pieces = lax.all_to_all(pieces, "y", 0, 0, tiled=True)
    grad_other = lax.ppermute(grad_own, "core", SWAP)

    share = whole(
        attended_grad_kernel,
        jax.ShapeDtypeStruct((n_frame, tokens, inner), BF16),
        place,
        weight_t,
        grad_own,
        grad_other,
        flops=2 * product,
    )
    weight_part = whole(
        weight_grad_kernel,
        jax.ShapeDtypeStruct(out_weight.shape, BF16),
        place,
        feature_rows,
        grad_own,
        grad_other,
        scratch=[pltpu.VMEM((halves, 2, width, inner), F32)],
        flops=2 * product,
    )
    near = lax.ppermute(share, "frame", [(i, i ^ 1) for i in range(n_frame)])
    weight_part, _, pieces = lax.optimization_barrier((weight_part, share, pieces))
    weight_part = weight_part.reshape(n_clip, inner // n_clip, -1)
    weight_part = lax.all_to_all(weight_part, CLIP, 0, 0, tiled=True)
    projected = pl.pallas_call(
        sum_kernel,
        out_shape=jax.ShapeDtypeStruct(pieces.shape[1:], BF16),
        compiler_params=pltpu.CompilerParams(vmem_limit_bytes=16 * 1024 * 1024),
        cost_estimate=pl.CostEstimate(flops=400 * product, bytes_accessed=2**20, transcendentals=0),
    )(pieces)
    projected, near = lax.optimization_barrier((projected, near))
    projected = lax.ppermute(projected, ("frame", "y"), there)
    near = (share.astype(F32) + near.astype(F32)).astype(BF16)
    far = lax.ppermute(near, "frame", [(i, n_frame - 1 - i) for i in range(n_frame)])

    weight_sum = jnp.sum(weight_part.astype(F32), axis=0).astype(BF16)
    _, near = lax.optimization_barrier((weight_sum, near))
    weight_grad = lax.all_to_all(copies(weight_sum, n_clip), CLIP, 0, 0, tiled=True)
    weight_grad = weight_grad.reshape(out_weight.shape)

    qkv_grad = whole(
        lambda *refs: attend_back_kernel(patches // n_frame, *refs),
        jax.ShapeDtypeStruct((steps, kinds, patches, inner), BF16),
        place,
        qkv_all,
        near,
        far,
        scratch=[
            pltpu.VMEM((frames, patches, inner), F32),
            pltpu.VMEM((frames, kinds, patches, inner), F32),
        ],
        flops=400 * product,
    )
    projected, qkv_grad = lax.optimization_barrier((projected, qkv_grad))
    projected = projected.T.reshape(residual.shape)
    block_out = (residual.astype(F32) + projected.astype(F32)).astype(BF16)
    qkv_grad = qkv_grad.transpose(0, 2, 1, 3).reshape(projections.shape)
    return (block_out, qkv_grad, weight_grad)


def solution(mesh):
    n_clip, n_frame, n_head = mesh.devices.shape
    fine = Mesh(mesh.devices.reshape(n_clip // 2, 2, n_frame, n_head // 2, 2), AXES)
    head = ("y", "core")
    in_specs = (
        P(CLIP, "frame", None, head),
        P(CLIP, "frame", None, None, head),
        P(head, "frame"),
        P(CLIP, "frame", None, head),
    )
    out_specs = (
        P(CLIP, "frame", None, head),
        P(CLIP, "frame", None, None, head),
        P(head, "frame"),
    )
    return jax.shard_map(local, mesh=fine, in_specs=in_specs, out_specs=out_specs, check_vma=False)
```

```python
import jax
import jax.numpy as jnp
from jax import lax
from jax.experimental import pallas as pl
from jax.experimental.pallas import tpu as pltpu
from jax.sharding import Mesh, PartitionSpec as P

HEAD_DIM = 128
AXES = ("x", "zl", "frame", "y", "core")
CLIP = ("x", "zl")
SWAP = ((0, 1), (1, 0))
F32 = jnp.float32
BF16 = jnp.bfloat16


def probabilities(queries, key_rows, patches):
    rows = queries.shape[0]
    scores = lax.dot_general(
        queries, key_rows, (((1,), (1,)), ((), ())), preferred_element_type=F32
    ) * (HEAD_DIM ** (-0.5))
    at = lax.broadcasted_iota(jnp.int32, (rows, rows), 0)
    to = lax.broadcasted_iota(jnp.int32, (rows, rows), 1)
    allowed = (at % patches == to % patches) & (at >= to)
    scores = jnp.where(allowed, scores, -jnp.inf)
    shifted = jnp.exp(scores - jnp.max(scores, axis=-1, keepdims=True))
    return shifted / jnp.sum(shifted, axis=-1, keepdims=True)


def block_of(part):
    return part.reshape(-1, part.shape[-1]).astype(BF16)


def attend_kernel(all_ref, rows_ref, sums_ref):
    n, tokens = rows_ref.shape[0], rows_ref.shape[1]
    frames, kinds, patches, width = all_ref.shape
    group = patches // n
    for at in range(0, width, HEAD_DIM):
        features = slice(at, at + HEAD_DIM)
        parts = [all_ref[:, kind, :, features].astype(F32) for kind in range(kinds)]
        for start in range(0, patches, group):
            span = slice(start, start + group)
            queries, key_rows, values = (block_of(part[:, span]) for part in parts)
            weights = probabilities(queries, key_rows, group).astype(BF16)
            attended = jnp.dot(weights, values, preferred_element_type=F32)
            sums_ref[:, span, features] = attended.reshape(frames, group, HEAD_DIM)
    rows_ref[...] = sums_ref[...].reshape(n, tokens, width).astype(BF16)


def slot(place_ref, frame, n):
    return lax.rem(2 * place_ref[0] + n // 2 + n - frame, n)


def project_block(weight, rows):
    flat = rows.reshape(-1, rows.shape[-1])
    return lax.dot_general(weight, flat, (((1,), (1,)), ((), ())), preferred_element_type=F32)


def project_other_kernel(place_ref, weight_ref, rows_ref, pieces_ref):
    n, tokens = rows_ref.shape[0], rows_ref.shape[1]
    halves = weight_ref.shape[0]
    for half in range(halves):
        block = project_block(weight_ref[half, 1 - place_ref[1]], rows_ref[...]).astype(BF16)
        for frame in range(n):
            pieces_ref[slot(place_ref, frame, n) * halves + half] = block[:, frame * tokens : (frame + 1) * tokens]


def project_own_kernel(place_ref, weight_ref, rows_ref, got_ref, pieces_ref):
    n, tokens = rows_ref.shape[0], rows_ref.shape[1]
    halves = weight_ref.shape[0]
    for half in range(halves):
        block = project_block(weight_ref[half, place_ref[1]], rows_ref[...])
        for frame in range(n):
            at = slot(place_ref, frame, n) * halves + half
            piece = block[:, frame * tokens : (frame + 1) * tokens] + got_ref[at].astype(F32)
            pieces_ref[at] = piece.astype(BF16)


def attended_grad_kernel(place_ref, weight_ref, own_ref, other_ref, out_ref):
    n, halves = out_ref.shape[0], weight_ref.shape[0]
    core = place_ref[1]
    for frame in range(n):
        total = None
        for half in range(halves):
            for grads, at in ((own_ref, core), (other_ref, 1 - core)):
                term = lax.dot_general(
                    grads[slot(place_ref, frame, n) * halves + half],
                    weight_ref[half, at],
                    (((0,), (0,)), ((), ())),
                    preferred_element_type=F32,
                )
                total = term if total is None else total + term
        out_ref[frame] = total.astype(BF16)


def weight_grad_kernel(place_ref, rows_ref, own_ref, other_ref, out_ref, sums_ref):
    n = rows_ref.shape[0]
    halves = sums_ref.shape[0]
    core = place_ref[1]
    for half in range(halves):
        for grads, at in ((own_ref, core), (other_ref, 1 - core)):
            total = None
            for frame in range(n):
                term = jnp.dot(
                    grads[slot(place_ref, frame, n) * halves + half], rows_ref[frame], preferred_element_type=F32
                )
                total = term if total is None else total + term
            sums_ref[half, at] = total
    out_ref[...] = sums_ref[...].reshape(-1, sums_ref.shape[-1]).T.astype(BF16)


def add_kernel(one_ref, two_ref, out_ref):
    out_ref[...] = (one_ref[...].astype(F32) + two_ref[...].astype(F32)).astype(BF16)


def sum_kernel(parts_ref, out_ref):
    total = parts_ref[0].astype(F32)
    for at in range(1, parts_ref.shape[0]):
        total = total + parts_ref[at].astype(F32)
    out_ref[...] = total.astype(BF16)


def attend_back_kernel(group, place_ref, all_ref, near_ref, far_ref, out_ref, grads_ref, sums_ref):
    frames, kinds, patches, width = all_ref.shape
    steps = out_ref.shape[0]
    total = near_ref[...].astype(F32) + far_ref[...].astype(F32)
    grads_ref[...] = total.reshape(frames, patches, width)
    score_scale = HEAD_DIM ** (-0.5)
    for at in range(0, width, HEAD_DIM):
        features = slice(at, at + HEAD_DIM)
        parts = [all_ref[:, kind, :, features].astype(F32) for kind in range(kinds)]
        for start in range(0, patches, group):
            span = slice(start, start + group)
            queries, key_rows, values = (block_of(part[:, span]) for part in parts)
            grad = block_of(grads_ref[:, span, features])
            probability = probabilities(queries, key_rows, group)
            prob_grad = lax.dot_general(
                grad, values, (((1,), (1,)), ((), ())), preferred_element_type=F32
            )
            row_dot = jnp.sum(probability * prob_grad, axis=-1, keepdims=True)
            score_grad = (probability * (prob_grad - row_dot)).astype(BF16)
            query_grad = jnp.dot(score_grad, key_rows, preferred_element_type=F32) * score_scale
            key_grad = (
                lax.dot_general(
                    score_grad, queries, (((0,), (0,)), ((), ())), preferred_element_type=F32
                )
                * score_scale
            )
            value_grad = lax.dot_general(
                probability.astype(BF16), grad, (((0,), (0,)), ((), ())), preferred_element_type=F32
            )
            for kind, value in enumerate((query_grad, key_grad, value_grad)):
                sums_ref[:, kind, span, features] = value.reshape(frames, group, HEAD_DIM)
    for step in range(steps):
        out_ref[step] = sums_ref[place_ref[0] * steps + step].astype(BF16)


def whole(kernel, out_shape, place, *operands, scratch=(), flops=0):
    several = isinstance(out_shape, (list, tuple))
    moved = sum(o.size * o.dtype.itemsize for o in operands)
    return pl.pallas_call(
        kernel,
        out_shape=out_shape,
        in_specs=[pl.BlockSpec(memory_space=pltpu.SMEM)]
        + [pl.BlockSpec(memory_space=pltpu.VMEM)] * len(operands),
        out_specs=[pl.BlockSpec(memory_space=pltpu.VMEM)] * len(out_shape)
        if several
        else pl.BlockSpec(memory_space=pltpu.VMEM),
        scratch_shapes=list(scratch),
        compiler_params=pltpu.CompilerParams(vmem_limit_bytes=16 * 1024 * 1024),
        cost_estimate=pl.CostEstimate(flops=flops, bytes_accessed=2 * moved, transcendentals=0),
    )(place, *operands)


def shifted(array, by, axis):
    n = lax.axis_size(axis)
    return lax.ppermute(array, axis, [(i, (i + by) % n) for i in range(n)])


def copies(array, n):
    return jnp.broadcast_to(array[None], (n, *array.shape))


def local(residual, projections, out_weight, out_grad):
    n_frame, n_y = lax.axis_size("frame"), lax.axis_size("y")
    n_clip = lax.axis_size("x") * lax.axis_size("zl")
    frame, core = lax.axis_index("frame"), lax.axis_index("core")
    place = jnp.stack([frame, core]).astype(jnp.int32)
    _, steps, patches, kinds, inner = projections.shape
    width = out_grad.shape[-1]
    frames = steps * n_frame
    tokens = steps * patches
    halves = n_y // n_frame
    product = 2 * n_frame * tokens * inner * width * halves

    there = [
        (
            f * n_y + y,
            (2 * f + n_frame // 2 - y // halves) % n_frame * n_y + halves * f + y % halves,
        )
        for f in range(n_frame)
        for y in range(n_y)
    ]
    back = [(b, a) for a, b in there]

    grad_moved = lax.ppermute(out_grad.reshape(tokens, width).T, ("frame", "y"), back)
    qkv_all = lax.all_gather(
        projections.reshape(projections.shape[1:]).transpose(0, 2, 1, 3), "frame", tiled=True
    )
    grad_moved, qkv_all = lax.optimization_barrier((grad_moved, qkv_all))
    grad_own = lax.all_to_all(copies(grad_moved, n_y), "y", 0, 0, tiled=True)

    feature_rows = pl.pallas_call(
        attend_kernel,
        out_shape=jax.ShapeDtypeStruct((n_frame, tokens, inner), BF16),
        scratch_shapes=[pltpu.VMEM((frames, patches, inner), F32)],
        compiler_params=pltpu.CompilerParams(vmem_limit_bytes=16 * 1024 * 1024),
        cost_estimate=pl.CostEstimate(flops=product, bytes_accessed=2**22, transcendentals=0),
    )(qkv_all)

    weight_t = out_weight.T.reshape(halves, 2, width, inner)
    piece_shape = jax.ShapeDtypeStruct((n_y, width, tokens), BF16)
    pieces_other = whole(
        project_other_kernel, piece_shape, place, weight_t, feature_rows, flops=product
    )
    pieces_got = lax.ppermute(pieces_other, "core", SWAP)
    pieces = whole(
        project_own_kernel, piece_shape, place, weight_t, feature_rows, pieces_got, flops=product
    )
    pieces, grad_own = lax.optimization_barrier((pieces, grad_own))
    pieces = lax.all_to_all(pieces, "y", 0, 0, tiled=True)
    grad_other = lax.ppermute(grad_own, "core", SWAP)

    share = whole(
        attended_grad_kernel,
        jax.ShapeDtypeStruct((n_frame, tokens, inner), BF16),
        place,
        weight_t,
        grad_own,
        grad_other,
        flops=2 * product,
    )
    weight_part = whole(
        weight_grad_kernel,
        jax.ShapeDtypeStruct(out_weight.shape, BF16),
        place,
        feature_rows,
        grad_own,
        grad_other,
        scratch=[pltpu.VMEM((halves, 2, width, inner), F32)],
        flops=2 * product,
    )
    near = lax.ppermute(share, "frame", [(i, i ^ 1) for i in range(n_frame)])
    weight_part, _, pieces = lax.optimization_barrier((weight_part, share, pieces))
    weight_part = weight_part.reshape(n_clip, inner // n_clip, -1)
    weight_part = lax.all_to_all(weight_part, CLIP, 0, 0, tiled=True)
    projected = pl.pallas_call(
        sum_kernel,
        out_shape=jax.ShapeDtypeStruct(pieces.shape[1:], BF16),
        compiler_params=pltpu.CompilerParams(vmem_limit_bytes=16 * 1024 * 1024),
        cost_estimate=pl.CostEstimate(flops=400 * product, bytes_accessed=2**20, transcendentals=0),
    )(pieces)
    projected, near = lax.optimization_barrier((projected, near))
    projected = lax.ppermute(projected, ("frame", "y"), there)
    near = pl.pallas_call(
        add_kernel,
        out_shape=jax.ShapeDtypeStruct(share.shape, BF16),
        compiler_params=pltpu.CompilerParams(vmem_limit_bytes=16 * 1024 * 1024),
        cost_estimate=pl.CostEstimate(flops=0, bytes_accessed=2**20, transcendentals=0),
    )(share, near)
    far = lax.ppermute(near, "frame", [(i, n_frame - 1 - i) for i in range(n_frame)])

    weight_sum = jnp.sum(weight_part.astype(F32), axis=0).astype(BF16)
    _, near = lax.optimization_barrier((weight_sum, near))
    weight_grad = lax.all_to_all(copies(weight_sum, n_clip), CLIP, 0, 0, tiled=True)
    weight_grad = weight_grad.reshape(out_weight.shape)

    qkv_grad = whole(
        lambda *refs: attend_back_kernel(patches // n_frame, *refs),
        jax.ShapeDtypeStruct((steps, kinds, patches, inner), BF16),
        place,
        qkv_all,
        near,
        far,
        scratch=[
            pltpu.VMEM((frames, patches, inner), F32),
            pltpu.VMEM((frames, kinds, patches, inner), F32),
        ],
        flops=400 * product,
    )
    projected, qkv_grad = lax.optimization_barrier((projected, qkv_grad))
    projected = projected.T.reshape(residual.shape)
    block_out = (residual.astype(F32) + projected.astype(F32)).astype(BF16)
    qkv_grad = qkv_grad.transpose(0, 2, 1, 3).reshape(projections.shape)
    return (block_out, qkv_grad, weight_grad)


def solution(mesh):
    n_clip, n_frame, n_head = mesh.devices.shape
    fine = Mesh(mesh.devices.reshape(n_clip // 2, 2, n_frame, n_head // 2, 2), AXES)
    head = ("y", "core")
    in_specs = (
        P(CLIP, "frame", None, head),
        P(CLIP, "frame", None, None, head),
        P(head, "frame"),
        P(CLIP, "frame", None, head),
    )
    out_specs = (
        P(CLIP, "frame", None, head),
        P(CLIP, "frame", None, None, head),
        P(head, "frame"),
    )
    return jax.shard_map(local, mesh=fine, in_specs=in_specs, out_specs=out_specs, check_vma=False)
```

```python
import jax
import jax.numpy as jnp
from jax import lax
from jax.experimental import pallas as pl
from jax.experimental.pallas import tpu as pltpu
from jax.sharding import Mesh, PartitionSpec as P

HEAD_DIM = 128
AXES = ("x", "zl", "frame", "y", "core")
CLIP = ("x", "zl")
SWAP = ((0, 1), (1, 0))
F32 = jnp.float32
BF16 = jnp.bfloat16


def probabilities(queries, key_rows, patches):
    rows = queries.shape[0]
    scores = lax.dot_general(
        queries, key_rows, (((1,), (1,)), ((), ())), preferred_element_type=F32
    ) * (HEAD_DIM ** (-0.5))
    at = lax.broadcasted_iota(jnp.int32, (rows, rows), 0)
    to = lax.broadcasted_iota(jnp.int32, (rows, rows), 1)
    allowed = (at % patches == to % patches) & (at >= to)
    scores = jnp.where(allowed, scores, -jnp.inf)
    shifted = jnp.exp(scores - jnp.max(scores, axis=-1, keepdims=True))
    return shifted / jnp.sum(shifted, axis=-1, keepdims=True)


def block_of(part):
    return part.reshape(-1, part.shape[-1]).astype(BF16)


def attend_kernel(all_ref, rows_ref, sums_ref):
    n, tokens = rows_ref.shape[0], rows_ref.shape[1]
    frames, kinds, patches, width = all_ref.shape
    group = patches // n
    for at in range(0, width, HEAD_DIM):
        features = slice(at, at + HEAD_DIM)
        parts = [all_ref[:, kind, :, features].astype(F32) for kind in range(kinds)]
        for start in range(0, patches, group):
            span = slice(start, start + group)
            queries, key_rows, values = (block_of(part[:, span]) for part in parts)
            weights = probabilities(queries, key_rows, group).astype(BF16)
            attended = jnp.dot(weights, values, preferred_element_type=F32)
            sums_ref[:, span, features] = attended.reshape(frames, group, HEAD_DIM)
    rows_ref[...] = sums_ref[...].reshape(n, tokens, width).astype(BF16)


def slot(place_ref, frame, n):
    return lax.rem(2 * place_ref[0] + n // 2 + n - frame, n)


def turn_kernel(array_ref, out_ref):
    out_ref[...] = array_ref[...].T


def project_block(weight, rows):
    flat = rows.reshape(-1, rows.shape[-1])
    return lax.dot_general(weight, flat, (((1,), (1,)), ((), ())), preferred_element_type=F32)


def project_other_kernel(place_ref, weight_ref, rows_ref, pieces_ref):
    n, tokens = rows_ref.shape[0], rows_ref.shape[1]
    halves = weight_ref.shape[0]
    for half in range(halves):
        block = project_block(weight_ref[half, 1 - place_ref[1]], rows_ref[...]).astype(BF16)
        for frame in range(n):
            pieces_ref[slot(place_ref, frame, n) * halves + half] = block[:, frame * tokens : (frame + 1) * tokens]


def project_own_kernel(place_ref, weight_ref, rows_ref, got_ref, pieces_ref):
    n, tokens = rows_ref.shape[0], rows_ref.shape[1]
    halves = weight_ref.shape[0]
    for half in range(halves):
        block = project_block(weight_ref[half, place_ref[1]], rows_ref[...])
        for frame in range(n):
            at = slot(place_ref, frame, n) * halves + half
            piece = block[:, frame * tokens : (frame + 1) * tokens] + got_ref[at].astype(F32)
            pieces_ref[at] = piece.astype(BF16)


def attended_grad_kernel(place_ref, weight_ref, own_ref, other_ref, out_ref):
    n, halves = out_ref.shape[0], weight_ref.shape[0]
    core = place_ref[1]
    for frame in range(n):
        total = None
        for half in range(halves):
            for grads, at in ((own_ref, core), (other_ref, 1 - core)):
                term = lax.dot_general(
                    grads[slot(place_ref, frame, n) * halves + half],
                    weight_ref[half, at],
                    (((0,), (0,)), ((), ())),
                    preferred_element_type=F32,
                )
                total = term if total is None else total + term
        out_ref[frame] = total.astype(BF16)


def weight_grad_kernel(place_ref, rows_ref, own_ref, other_ref, out_ref, sums_ref):
    n = rows_ref.shape[0]
    halves = sums_ref.shape[0]
    core = place_ref[1]
    for half in range(halves):
        for grads, at in ((own_ref, core), (other_ref, 1 - core)):
            total = None
            for frame in range(n):
                term = jnp.dot(
                    grads[slot(place_ref, frame, n) * halves + half], rows_ref[frame], preferred_element_type=F32
                )
                total = term if total is None else total + term
            sums_ref[half, at] = total
    out_ref[...] = sums_ref[...].reshape(-1, sums_ref.shape[-1]).T.astype(BF16)


def add_kernel(one_ref, two_ref, out_ref):
    out_ref[...] = (one_ref[...].astype(F32) + two_ref[...].astype(F32)).astype(BF16)


def sum_kernel(parts_ref, out_ref):
    total = parts_ref[0].astype(F32)
    for at in range(1, parts_ref.shape[0]):
        total = total + parts_ref[at].astype(F32)
    out_ref[...] = total.astype(BF16)


def attend_back_kernel(group, place_ref, all_ref, near_ref, far_ref, out_ref, grads_ref, sums_ref):
    frames, kinds, patches, width = all_ref.shape
    steps = out_ref.shape[0]
    total = near_ref[...].astype(F32) + far_ref[...].astype(F32)
    grads_ref[...] = total.reshape(frames, patches, width)
    score_scale = HEAD_DIM ** (-0.5)
    for at in range(0, width, HEAD_DIM):
        features = slice(at, at + HEAD_DIM)
        parts = [all_ref[:, kind, :, features].astype(F32) for kind in range(kinds)]
        for start in range(0, patches, group):
            span = slice(start, start + group)
            queries, key_rows, values = (block_of(part[:, span]) for part in parts)
            grad = block_of(grads_ref[:, span, features])
            probability = probabilities(queries, key_rows, group)
            prob_grad = lax.dot_general(
                grad, values, (((1,), (1,)), ((), ())), preferred_element_type=F32
            )
            row_dot = jnp.sum(probability * prob_grad, axis=-1, keepdims=True)
            score_grad = (probability * (prob_grad - row_dot)).astype(BF16)
            query_grad = jnp.dot(score_grad, key_rows, preferred_element_type=F32) * score_scale
            key_grad = (
                lax.dot_general(
                    score_grad, queries, (((0,), (0,)), ((), ())), preferred_element_type=F32
                )
                * score_scale
            )
            value_grad = lax.dot_general(
                probability.astype(BF16), grad, (((0,), (0,)), ((), ())), preferred_element_type=F32
            )
            for kind, value in enumerate((query_grad, key_grad, value_grad)):
                sums_ref[:, kind, span, features] = value.reshape(frames, group, HEAD_DIM)
    for step in range(steps):
        out_ref[step] = sums_ref[place_ref[0] * steps + step].astype(BF16)


def whole(kernel, out_shape, place, *operands, scratch=(), flops=0):
    several = isinstance(out_shape, (list, tuple))
    moved = sum(o.size * o.dtype.itemsize for o in operands)
    return pl.pallas_call(
        kernel,
        out_shape=out_shape,
        in_specs=[pl.BlockSpec(memory_space=pltpu.SMEM)]
        + [pl.BlockSpec(memory_space=pltpu.VMEM)] * len(operands),
        out_specs=[pl.BlockSpec(memory_space=pltpu.VMEM)] * len(out_shape)
        if several
        else pl.BlockSpec(memory_space=pltpu.VMEM),
        scratch_shapes=list(scratch),
        compiler_params=pltpu.CompilerParams(vmem_limit_bytes=16 * 1024 * 1024),
        cost_estimate=pl.CostEstimate(flops=flops, bytes_accessed=2 * moved, transcendentals=0),
    )(place, *operands)


def shifted(array, by, axis):
    n = lax.axis_size(axis)
    return lax.ppermute(array, axis, [(i, (i + by) % n) for i in range(n)])


def copies(array, n):
    return jnp.broadcast_to(array[None], (n, *array.shape))


def local(residual, projections, out_weight, out_grad):
    n_frame, n_y = lax.axis_size("frame"), lax.axis_size("y")
    n_clip = lax.axis_size("x") * lax.axis_size("zl")
    frame, core = lax.axis_index("frame"), lax.axis_index("core")
    place = jnp.stack([frame, core]).astype(jnp.int32)
    _, steps, patches, kinds, inner = projections.shape
    width = out_grad.shape[-1]
    frames = steps * n_frame
    tokens = steps * patches
    halves = n_y // n_frame
    product = 2 * n_frame * tokens * inner * width * halves

    there = [
        (
            f * n_y + y,
            (2 * f + n_frame // 2 - y // halves) % n_frame * n_y + halves * f + y % halves,
        )
        for f in range(n_frame)
        for y in range(n_y)
    ]
    back = [(b, a) for a, b in there]

    grad_t = pl.pallas_call(
        turn_kernel,
        out_shape=jax.ShapeDtypeStruct((width, tokens), BF16),
        cost_estimate=pl.CostEstimate(flops=0, bytes_accessed=2**17, transcendentals=0),
    )(out_grad.reshape(tokens, width))
    grad_moved = lax.ppermute(grad_t, ("frame", "y"), back)
    qkv_all = lax.all_gather(
        projections.reshape(projections.shape[1:]).transpose(0, 2, 1, 3), "frame", tiled=True
    )
    grad_moved, qkv_all = lax.optimization_barrier((grad_moved, qkv_all))
    grad_own = lax.all_to_all(copies(grad_moved, n_y), "y", 0, 0, tiled=True)

    feature_rows = pl.pallas_call(
        attend_kernel,
        out_shape=jax.ShapeDtypeStruct((n_frame, tokens, inner), BF16),
        scratch_shapes=[pltpu.VMEM((frames, patches, inner), F32)],
        compiler_params=pltpu.CompilerParams(vmem_limit_bytes=16 * 1024 * 1024),
        cost_estimate=pl.CostEstimate(flops=product, bytes_accessed=2**22, transcendentals=0),
    )(qkv_all)

    weight_t = out_weight.T.reshape(halves, 2, width, inner)
    piece_shape = jax.ShapeDtypeStruct((n_y, width, tokens), BF16)
    pieces_other = whole(
        project_other_kernel, piece_shape, place, weight_t, feature_rows, flops=product
    )
    pieces_got = lax.ppermute(pieces_other, "core", SWAP)
    pieces = whole(
        project_own_kernel, piece_shape, place, weight_t, feature_rows, pieces_got, flops=product
    )
    pieces, grad_own = lax.optimization_barrier((pieces, grad_own))
    pieces = lax.all_to_all(pieces, "y", 0, 0, tiled=True)
    grad_other = lax.ppermute(grad_own, "core", SWAP)

    share = whole(
        attended_grad_kernel,
        jax.ShapeDtypeStruct((n_frame, tokens, inner), BF16),
        place,
        weight_t,
        grad_own,
        grad_other,
        flops=2 * product,
    )
    weight_part = whole(
        weight_grad_kernel,
        jax.ShapeDtypeStruct(out_weight.shape, BF16),
        place,
        feature_rows,
        grad_own,
        grad_other,
        scratch=[pltpu.VMEM((halves, 2, width, inner), F32)],
        flops=2 * product,
    )
    near = lax.ppermute(share, "frame", [(i, i ^ 1) for i in range(n_frame)])
    weight_part, _, pieces = lax.optimization_barrier((weight_part, share, pieces))
    weight_part = weight_part.reshape(n_clip, inner // n_clip, -1)
    weight_part = lax.all_to_all(weight_part, CLIP, 0, 0, tiled=True)
    projected = pl.pallas_call(
        sum_kernel,
        out_shape=jax.ShapeDtypeStruct(pieces.shape[1:], BF16),
        compiler_params=pltpu.CompilerParams(vmem_limit_bytes=16 * 1024 * 1024),
        cost_estimate=pl.CostEstimate(flops=400 * product, bytes_accessed=2**20, transcendentals=0),
    )(pieces)
    projected, near = lax.optimization_barrier((projected, near))
    projected = lax.ppermute(projected, ("frame", "y"), there)
    near = pl.pallas_call(
        add_kernel,
        out_shape=jax.ShapeDtypeStruct(share.shape, BF16),
        compiler_params=pltpu.CompilerParams(vmem_limit_bytes=16 * 1024 * 1024),
        cost_estimate=pl.CostEstimate(flops=0, bytes_accessed=2**20, transcendentals=0),
    )(share, near)
    far = lax.ppermute(near, "frame", [(i, n_frame - 1 - i) for i in range(n_frame)])

    weight_sum = jnp.sum(weight_part.astype(F32), axis=0).astype(BF16)
    _, near = lax.optimization_barrier((weight_sum, near))
    weight_grad = lax.all_to_all(copies(weight_sum, n_clip), CLIP, 0, 0, tiled=True)
    weight_grad = weight_grad.reshape(out_weight.shape)

    qkv_grad = whole(
        lambda *refs: attend_back_kernel(patches // n_frame, *refs),
        jax.ShapeDtypeStruct((steps, kinds, patches, inner), BF16),
        place,
        qkv_all,
        near,
        far,
        scratch=[
            pltpu.VMEM((frames, patches, inner), F32),
            pltpu.VMEM((frames, kinds, patches, inner), F32),
        ],
        flops=400 * product,
    )
    projected, qkv_grad = lax.optimization_barrier((projected, qkv_grad))
    projected = projected.T.reshape(residual.shape)
    block_out = (residual.astype(F32) + projected.astype(F32)).astype(BF16)
    qkv_grad = qkv_grad.transpose(0, 2, 1, 3).reshape(projections.shape)
    return (block_out, qkv_grad, weight_grad)


def solution(mesh):
    n_clip, n_frame, n_head = mesh.devices.shape
    fine = Mesh(mesh.devices.reshape(n_clip // 2, 2, n_frame, n_head // 2, 2), AXES)
    head = ("y", "core")
    in_specs = (
        P(CLIP, "frame", None, head),
        P(CLIP, "frame", None, None, head),
        P(head, "frame"),
        P(CLIP, "frame", None, head),
    )
    out_specs = (
        P(CLIP, "frame", None, head),
        P(CLIP, "frame", None, None, head),
        P(head, "frame"),
    )
    return jax.shard_map(local, mesh=fine, in_specs=in_specs, out_specs=out_specs, check_vma=False)
```

```python
import jax
import jax.numpy as jnp
from jax import lax
from jax.experimental import pallas as pl
from jax.experimental.pallas import tpu as pltpu
from jax.sharding import Mesh, PartitionSpec as P

HEAD_DIM = 128
AXES = ("x", "zl", "frame", "y", "core")
CLIP = ("x", "zl")
SWAP = ((0, 1), (1, 0))
F32 = jnp.float32
BF16 = jnp.bfloat16


def probabilities(queries, key_rows, patches):
    rows = queries.shape[0]
    scores = lax.dot_general(
        queries, key_rows, (((1,), (1,)), ((), ())), preferred_element_type=F32
    ) * (HEAD_DIM ** (-0.5))
    at = lax.broadcasted_iota(jnp.int32, (rows, rows), 0)
    to = lax.broadcasted_iota(jnp.int32, (rows, rows), 1)
    allowed = (at % patches == to % patches) & (at >= to)
    scores = jnp.where(allowed, scores, -jnp.inf)
    shifted = jnp.exp(scores - jnp.max(scores, axis=-1, keepdims=True))
    return shifted / jnp.sum(shifted, axis=-1, keepdims=True)


def block_of(part):
    return part.reshape(-1, part.shape[-1]).astype(BF16)


def attend_kernel(all_ref, rows_ref, sums_ref):
    n, tokens = rows_ref.shape[0], rows_ref.shape[1]
    frames, kinds, patches, width = all_ref.shape
    group = patches // n
    for at in range(0, width, HEAD_DIM):
        features = slice(at, at + HEAD_DIM)
        parts = [all_ref[:, kind, :, features].astype(F32) for kind in range(kinds)]
        for start in range(0, patches, group):
            span = slice(start, start + group)
            queries, key_rows, values = (block_of(part[:, span]) for part in parts)
            weights = probabilities(queries, key_rows, group).astype(BF16)
            attended = jnp.dot(weights, values, preferred_element_type=F32)
            sums_ref[:, span, features] = attended.reshape(frames, group, HEAD_DIM)
    rows_ref[...] = sums_ref[...].reshape(n, tokens, width).astype(BF16)


def slot(place_ref, frame, n):
    return lax.rem(2 * place_ref[0] + n // 2 + n - frame, n)


def project_block(weight, rows):
    flat = rows.reshape(-1, rows.shape[-1])
    return lax.dot_general(weight, flat, (((1,), (1,)), ((), ())), preferred_element_type=F32)


def project_other_kernel(place_ref, weight_ref, rows_ref, pieces_ref):
    n, tokens = rows_ref.shape[0], rows_ref.shape[1]
    halves = weight_ref.shape[0]
    for half in range(halves):
        block = project_block(weight_ref[half, 1 - place_ref[1]], rows_ref[...]).astype(BF16)
        for frame in range(n):
            pieces_ref[slot(place_ref, frame, n) * halves + half] = block[:, frame * tokens : (frame + 1) * tokens]


def project_own_kernel(place_ref, weight_ref, rows_ref, got_ref, pieces_ref):
    n, tokens = rows_ref.shape[0], rows_ref.shape[1]
    halves = weight_ref.shape[0]
    for half in range(halves):
        block = project_block(weight_ref[half, place_ref[1]], rows_ref[...])
        for frame in range(n):
            at = slot(place_ref, frame, n) * halves + half
            piece = block[:, frame * tokens : (frame + 1) * tokens] + got_ref[at].astype(F32)
            pieces_ref[at] = piece.astype(BF16)


def share_own_kernel(place_ref, weight_ref, own_ref, out_ref):
    n, halves = out_ref.shape[0], weight_ref.shape[0]
    for frame in range(n):
        total = None
        for half in range(halves):
            term = lax.dot_general(
                own_ref[slot(place_ref, frame, n) * halves + half],
                weight_ref[half, place_ref[1]],
                (((0,), (0,)), ((), ())),
                preferred_element_type=F32,
            )
            total = term if total is None else total + term
        out_ref[frame] = total


def share_other_kernel(place_ref, weight_ref, other_ref, first_ref, out_ref):
    n, halves = out_ref.shape[0], weight_ref.shape[0]
    for frame in range(n):
        total = first_ref[frame]
        for half in range(halves):
            total = total + lax.dot_general(
                other_ref[slot(place_ref, frame, n) * halves + half],
                weight_ref[half, 1 - place_ref[1]],
                (((0,), (0,)), ((), ())),
                preferred_element_type=F32,
            )
        out_ref[frame] = total.astype(BF16)


def weight_grad_kernel(place_ref, rows_ref, own_ref, other_ref, out_ref, sums_ref):
    n = rows_ref.shape[0]
    halves = sums_ref.shape[0]
    core = place_ref[1]
    for half in range(halves):
        for grads, at in ((own_ref, core), (other_ref, 1 - core)):
            total = None
            for frame in range(n):
                term = jnp.dot(
                    grads[slot(place_ref, frame, n) * halves + half], rows_ref[frame], preferred_element_type=F32
                )
                total = term if total is None else total + term
            sums_ref[half, at] = total
    out_ref[...] = sums_ref[...].reshape(-1, sums_ref.shape[-1]).T.astype(BF16)


def add_kernel(one_ref, two_ref, out_ref):
    out_ref[...] = (one_ref[...].astype(F32) + two_ref[...].astype(F32)).astype(BF16)


def sum_kernel(parts_ref, out_ref):
    total = parts_ref[0].astype(F32)
    for at in range(1, parts_ref.shape[0]):
        total = total + parts_ref[at].astype(F32)
    out_ref[...] = total.astype(BF16)


def attend_back_kernel(group, place_ref, all_ref, near_ref, far_ref, out_ref, grads_ref, sums_ref):
    frames, kinds, patches, width = all_ref.shape
    steps = out_ref.shape[0]
    total = near_ref[...].astype(F32) + far_ref[...].astype(F32)
    grads_ref[...] = total.reshape(frames, patches, width)
    score_scale = HEAD_DIM ** (-0.5)
    for at in range(0, width, HEAD_DIM):
        features = slice(at, at + HEAD_DIM)
        parts = [all_ref[:, kind, :, features].astype(F32) for kind in range(kinds)]
        for start in range(0, patches, group):
            span = slice(start, start + group)
            queries, key_rows, values = (block_of(part[:, span]) for part in parts)
            grad = block_of(grads_ref[:, span, features])
            probability = probabilities(queries, key_rows, group)
            prob_grad = lax.dot_general(
                grad, values, (((1,), (1,)), ((), ())), preferred_element_type=F32
            )
            row_dot = jnp.sum(probability * prob_grad, axis=-1, keepdims=True)
            score_grad = (probability * (prob_grad - row_dot)).astype(BF16)
            query_grad = jnp.dot(score_grad, key_rows, preferred_element_type=F32) * score_scale
            key_grad = (
                lax.dot_general(
                    score_grad, queries, (((0,), (0,)), ((), ())), preferred_element_type=F32
                )
                * score_scale
            )
            value_grad = lax.dot_general(
                probability.astype(BF16), grad, (((0,), (0,)), ((), ())), preferred_element_type=F32
            )
            for kind, value in enumerate((query_grad, key_grad, value_grad)):
                sums_ref[:, kind, span, features] = value.reshape(frames, group, HEAD_DIM)
    for step in range(steps):
        out_ref[step] = sums_ref[place_ref[0] * steps + step].astype(BF16)


def whole(kernel, out_shape, place, *operands, scratch=(), flops=0):
    several = isinstance(out_shape, (list, tuple))
    moved = sum(o.size * o.dtype.itemsize for o in operands)
    return pl.pallas_call(
        kernel,
        out_shape=out_shape,
        in_specs=[pl.BlockSpec(memory_space=pltpu.SMEM)]
        + [pl.BlockSpec(memory_space=pltpu.VMEM)] * len(operands),
        out_specs=[pl.BlockSpec(memory_space=pltpu.VMEM)] * len(out_shape)
        if several
        else pl.BlockSpec(memory_space=pltpu.VMEM),
        scratch_shapes=list(scratch),
        compiler_params=pltpu.CompilerParams(vmem_limit_bytes=16 * 1024 * 1024),
        cost_estimate=pl.CostEstimate(flops=flops, bytes_accessed=2 * moved, transcendentals=0),
    )(place, *operands)


def shifted(array, by, axis):
    n = lax.axis_size(axis)
    return lax.ppermute(array, axis, [(i, (i + by) % n) for i in range(n)])


def copies(array, n):
    return jnp.broadcast_to(array[None], (n, *array.shape))


def local(residual, projections, out_weight, out_grad):
    n_frame, n_y = lax.axis_size("frame"), lax.axis_size("y")
    n_clip = lax.axis_size("x") * lax.axis_size("zl")
    frame, core = lax.axis_index("frame"), lax.axis_index("core")
    place = jnp.stack([frame, core]).astype(jnp.int32)
    _, steps, patches, kinds, inner = projections.shape
    width = out_grad.shape[-1]
    frames = steps * n_frame
    tokens = steps * patches
    halves = n_y // n_frame
    product = 2 * n_frame * tokens * inner * width * halves

    there = [
        (
            f * n_y + y,
            (2 * f + n_frame // 2 - y // halves) % n_frame * n_y + halves * f + y % halves,
        )
        for f in range(n_frame)
        for y in range(n_y)
    ]
    back = [(b, a) for a, b in there]

    grad_moved = lax.ppermute(out_grad.reshape(tokens, width).T, ("frame", "y"), back)
    qkv_all = lax.all_gather(
        projections.reshape(projections.shape[1:]).transpose(0, 2, 1, 3), "frame", tiled=True
    )
    grad_moved, qkv_all = lax.optimization_barrier((grad_moved, qkv_all))
    grad_own = lax.all_to_all(copies(grad_moved, n_y), "y", 0, 0, tiled=True)

    feature_rows = pl.pallas_call(
        attend_kernel,
        out_shape=jax.ShapeDtypeStruct((n_frame, tokens, inner), BF16),
        scratch_shapes=[pltpu.VMEM((frames, patches, inner), F32)],
        compiler_params=pltpu.CompilerParams(vmem_limit_bytes=16 * 1024 * 1024),
        cost_estimate=pl.CostEstimate(flops=product, bytes_accessed=2**22, transcendentals=0),
    )(qkv_all)

    weight_t = out_weight.T.reshape(halves, 2, width, inner)
    piece_shape = jax.ShapeDtypeStruct((n_y, width, tokens), BF16)
    pieces_other = whole(
        project_other_kernel, piece_shape, place, weight_t, feature_rows, flops=product
    )
    pieces_got = lax.ppermute(pieces_other, "core", SWAP)
    pieces = whole(
        project_own_kernel, piece_shape, place, weight_t, feature_rows, pieces_got, flops=product
    )
    pieces, grad_own = lax.optimization_barrier((pieces, grad_own))
    pieces = lax.all_to_all(pieces, "y", 0, 0, tiled=True)
    grad_other = lax.ppermute(grad_own, "core", SWAP)

    share = whole(
        share_own_kernel,
        jax.ShapeDtypeStruct((n_frame, tokens, inner), F32),
        place,
        weight_t,
        grad_own,
        flops=product,
    )
    share = whole(
        share_other_kernel,
        jax.ShapeDtypeStruct((n_frame, tokens, inner), BF16),
        place,
        weight_t,
        grad_other,
        share,
        flops=product,
    )
    weight_part = whole(
        weight_grad_kernel,
        jax.ShapeDtypeStruct(out_weight.shape, BF16),
        place,
        feature_rows,
        grad_own,
        grad_other,
        scratch=[pltpu.VMEM((halves, 2, width, inner), F32)],
        flops=2 * product,
    )
    near = lax.ppermute(share, "frame", [(i, i ^ 1) for i in range(n_frame)])
    weight_part, _, pieces = lax.optimization_barrier((weight_part, share, pieces))
    weight_part = weight_part.reshape(n_clip, inner // n_clip, -1)
    weight_part = lax.all_to_all(weight_part, CLIP, 0, 0, tiled=True)
    projected = pl.pallas_call(
        sum_kernel,
        out_shape=jax.ShapeDtypeStruct(pieces.shape[1:], BF16),
        compiler_params=pltpu.CompilerParams(vmem_limit_bytes=16 * 1024 * 1024),
        cost_estimate=pl.CostEstimate(flops=400 * product, bytes_accessed=2**20, transcendentals=0),
    )(pieces)
    projected, near = lax.optimization_barrier((projected, near))
    projected = lax.ppermute(projected, ("frame", "y"), there)
    near = pl.pallas_call(
        add_kernel,
        out_shape=jax.ShapeDtypeStruct(share.shape, BF16),
        compiler_params=pltpu.CompilerParams(vmem_limit_bytes=16 * 1024 * 1024),
        cost_estimate=pl.CostEstimate(flops=0, bytes_accessed=2**20, transcendentals=0),
    )(share, near)
    far = lax.ppermute(near, "frame", [(i, n_frame - 1 - i) for i in range(n_frame)])

    weight_sum = jnp.sum(weight_part.astype(F32), axis=0).astype(BF16)
    _, near = lax.optimization_barrier((weight_sum, near))
    weight_grad = lax.all_to_all(copies(weight_sum, n_clip), CLIP, 0, 0, tiled=True)
    weight_grad = weight_grad.reshape(out_weight.shape)

    qkv_grad = whole(
        lambda *refs: attend_back_kernel(patches // n_frame, *refs),
        jax.ShapeDtypeStruct((steps, kinds, patches, inner), BF16),
        place,
        qkv_all,
        near,
        far,
        scratch=[
            pltpu.VMEM((frames, patches, inner), F32),
            pltpu.VMEM((frames, kinds, patches, inner), F32),
        ],
        flops=400 * product,
    )
    projected, qkv_grad = lax.optimization_barrier((projected, qkv_grad))
    projected = projected.T.reshape(residual.shape)
    block_out = (residual.astype(F32) + projected.astype(F32)).astype(BF16)
    qkv_grad = qkv_grad.transpose(0, 2, 1, 3).reshape(projections.shape)
    return (block_out, qkv_grad, weight_grad)


def solution(mesh):
    n_clip, n_frame, n_head = mesh.devices.shape
    fine = Mesh(mesh.devices.reshape(n_clip // 2, 2, n_frame, n_head // 2, 2), AXES)
    head = ("y", "core")
    in_specs = (
        P(CLIP, "frame", None, head),
        P(CLIP, "frame", None, None, head),
        P(head, "frame"),
        P(CLIP, "frame", None, head),
    )
    out_specs = (
        P(CLIP, "frame", None, head),
        P(CLIP, "frame", None, None, head),
        P(head, "frame"),
    )
    return jax.shard_map(local, mesh=fine, in_specs=in_specs, out_specs=out_specs, check_vma=False)
```
